32 devices in a mesh: head: 4 (over z), vocab: 8 (over y, x, core).
Axes of the slice: x: 2, y: 2, z: 4, core: 2. Of those that a mesh axis runs over, the one named last changes fastest.
Arguments:
- queries: bfloat16 [16, 8192], P(None, 'head')
- key_cache: bfloat16 [256, 1024], P('vocab', 'head')
- value_cache: bfloat16 [256, 1024], P('vocab', 'head'), may hold values from -6 to 6
- visible_len: int32 [16], replicated, may hold values from 128 to 241
- targets: int32 [16], replicated, may hold values from 0 to 28671
- final_scale: float32 [16], replicated, may hold values from 4 to 40
- w_out: bfloat16 [8192, 8192], P('head', 'vocab'), may hold values from -0.5 to 0.5
- unembed: bfloat16 [8192, 28672], P(None, ('head', 'vocab'))
Outputs:
- target_logit: float32 [64, 16], replicated
- log_norm: float32 [64, 16], replicated
The draws below stay inside these ranges and needn't reach their ends.
All inputs are finite; a program needn't handle non-finite values.
Results may differ from the reference program's by a relative error of at most 0.0043.
Values may be sent and summed in bfloat16 or wider, within the bound.
A program may use at most 128 MiB of HBM per device.

```python
import jax
import jax.numpy as jnp
from jax import lax

D = 8192
H = 64
KVH = 8
HD = 128
VOC_DEV = 896
QRY = 16
CTX = 256
VOCAB = 28672
N_HEAD = 4
N_VOCAB = 8


key_spread = 0.0625


query_spread = 16.0


def shared_keys(key):
    entries = jax.random.truncated_normal(jax.random.fold_in(key, 101), -6.0, 6.0, (CTX, KVH * HD), jnp.float32)
    return entries


def draw_key_cache(key, part):
    return (key_spread * shared_keys(key)).astype(jnp.bfloat16)


def draw_queries(key, part):
    entries = query_spread * jax.random.truncated_normal(jax.random.fold_in(key, 103), -6.0, 6.0, (QRY, H * HD), jnp.float32)
    return entries.astype(jnp.bfloat16)


def draw_final_scale(key, part):
    uniform_draw = jax.random.uniform(jax.random.fold_in(key, 104), (QRY,), jnp.float32)
    spread = 4.0 * jnp.exp(uniform_draw * jnp.log(10.0))
    return spread


def draw_unembed(key, part):
    col_draw = jax.random.uniform(jax.random.fold_in(key, 105), (1, VOCAB), jnp.float32)
    col_scale = jnp.exp(jnp.log(0.25) + col_draw * jnp.log(32.0))
    entries = jax.random.truncated_normal(jax.random.fold_in(key, 108), -6.0, 6.0, (D, VOCAB), jnp.float32)
    return (entries * col_scale * D ** (-0.5)).astype(jnp.bfloat16)


def with_ends(values, stream_key, low, high):
    extent = values.shape
    place = [jax.random.randint(jax.random.fold_in(stream_key, axis), (), 0, extent[axis]) for axis in range(len(extent))]
    values = values.at[tuple(place)].set(low)
    longest = extent.index(max(extent))
    place[longest] = (place[longest] + 1) % extent[longest]
    return values.at[tuple(place)].set(high)


def block_levels(key, dims, cuts, smallest, top_value):
    loudness, own = 1.0, jax.random.fold_in(key, 6)
    for dim, blocks in cuts:
        draws = jnp.exp(jax.random.uniform(jax.random.fold_in(own, dim), (blocks,), jnp.float32, smallest / len(cuts), top_value / len(cuts)))
        loudness = loudness * jnp.repeat(draws, dims[dim] // blocks).reshape([-1 if axis == dim else 1 for axis in range(len(dims))])
    return loudness


def centred(key, shape, deviation, bound, shards=(), kind=jnp.bfloat16):
    drawn = deviation * jax.random.normal(key, shape, jnp.float32)
    if shards:
        drawn = drawn * block_levels(key, shape, shards, -0.22, 0.18)
    return jnp.clip(drawn, -bound, bound).astype(kind)


def setup_inputs(seed: int = 0) -> dict:
    seeds = jax.random.split(jax.random.key(seed), 9)
    queries = draw_queries(jax.random.fold_in(seeds[8], 71), 0)
    key_cache = draw_key_cache(jax.random.fold_in(seeds[8], 71), 0)
    value_cache = centred(seeds[2], (CTX, KVH * HD), 1.0, 6.0, ((0, 8), (1, 4)))
    visible_len = with_ends(jax.random.randint(seeds[3], (QRY,), CTX // 2, CTX - QRY + 2), jax.random.fold_in(seeds[3], 1), CTX // 2, (CTX - QRY + 2) - 1).astype(jnp.int32)
    targets = with_ends(jax.random.randint(seeds[4], (QRY,), 0, VOCAB), jax.random.fold_in(seeds[4], 1), 0, VOCAB - 1).astype(jnp.int32)
    final_scale = draw_final_scale(jax.random.fold_in(seeds[8], 71), 0)
    w_out = centred(seeds[6], (H * HD, D), HD ** -0.5, 0.5, ((0, 4), (1, 8)))
    unembed = draw_unembed(jax.random.fold_in(seeds[8], 71), 0)
    return dict(queries=queries, key_cache=key_cache, value_cache=value_cache, visible_len=visible_len, targets=targets, final_scale=final_scale, w_out=w_out, unembed=unembed)


NEG_FILL = -1e30


def reference(queries, key_cache, value_cache, visible_len, targets, final_scale, w_out, unembed):
    context = key_cache.shape[0]
    query_count = queries.shape[0]
    group_size = H // KVH
    qgrid = queries.astype(jnp.float32).reshape(query_count, KVH, group_size, HD)
    kgrid = key_cache.astype(jnp.float32).reshape(context, KVH, HD)
    vgrid = value_cache.astype(jnp.float32).reshape(context, KVH, HD)
    scores = jnp.einsum("sngd,knd->ngsk", qgrid, kgrid, precision=lax.Precision.HIGHEST) * (HD ** -0.5)
    key_pos = jnp.arange(context, dtype=jnp.int32)
    query_pos = (context - query_count + jnp.arange(query_count, dtype=jnp.int32)).astype(jnp.int32)
    visible = (key_pos[None, :] <= query_pos[:, None]) & (key_pos[None, :] > (query_pos - visible_len)[:, None])
    masked = jnp.where(visible, scores, NEG_FILL)
    row_peak = jnp.max(masked, axis=-1)
    weights = jnp.where(visible, jnp.exp(masked - row_peak[..., None]), 0.0)
    row_total = jnp.sum(weights, axis=-1)
    summed = jnp.einsum("ngsk,knd->ngsd", weights, vgrid, precision=lax.Precision.HIGHEST)
    mixed = (summed / row_total[..., None]).astype(jnp.bfloat16).reshape(H, query_count, HD)
    projection = w_out.astype(jnp.float32).reshape(H, HD, D)
    contrib = jnp.einsum("hse,hed->hsd", mixed.astype(jnp.float32), projection, precision=lax.Precision.HIGHEST)
    scaled = (contrib * final_scale[None, :, None]).astype(jnp.bfloat16).reshape(H * query_count, D)
    block_width = VOC_DEV * N_VOCAB

    def vocab_step(running, block_index):
        old_peak, old_total, picked = running
        first_col = (block_index * block_width).astype(jnp.int32)
        weight_cols = lax.dynamic_slice_in_dim(unembed, first_col, block_width, 1)
        logits = jnp.dot(scaled, weight_cols, preferred_element_type=jnp.float32).reshape(H, query_count, block_width)
        col_index = first_col + jnp.arange(block_width, dtype=jnp.int32)
        target_hits = (targets[:, None] == col_index[None, :]).astype(logits.dtype)
        picked = picked + jnp.sum(logits * target_hits[None], axis=-1)
        new_peak = jnp.maximum(old_peak, jnp.max(logits, axis=-1))
        new_total = old_total * jnp.exp(old_peak - new_peak) + jnp.sum(jnp.exp(logits - new_peak[..., None]), axis=-1)
        return (new_peak, new_total, picked), None

    initial = (jnp.full((H, query_count), NEG_FILL, jnp.float32), jnp.zeros((H, query_count), jnp.float32), jnp.zeros((H, query_count), jnp.float32))
    (global_peak, global_total, target_logit), _ = lax.scan(vocab_step, initial, jnp.arange(N_HEAD, dtype=jnp.int32))
    return target_logit, global_peak + jnp.log(global_total)
```

```python
import functools

import jax
import jax.numpy as jnp
from jax import lax
from jax.experimental import pallas as pl
from jax.experimental.pallas import tpu as pltpu
from jax.sharding import PartitionSpec as P

H = 64
KVH = 8
HD = 128
GROUP = H // KVH
NEG_FILL = -1e30
MESH = pl.DeviceIdType.MESH
F32 = jnp.float32
BF16 = jnp.bfloat16


def column_tiles(width, tile=256):
    return [(at, min(tile, width - at)) for at in range(0, width, tile)]


def kernel(
    n_h, n_v,
    vis_ref, tgt_ref, fs_ref, q_ref, k_ref, v_ref, w_hbm, u_hbm,
    tl_ref, ln_ref,
    w_buf, u_buf, blocks, acc, kbuf, vbuf, cols, st_all, st_z,
    w_sem, u_sem, kv_send, kv_recv, recv, z_send, x_send, y_send, x_fwd, y_fwd, sib_send,
    st_send, st_recv, sz_send, sz_recv,
):
    z = lax.axis_index("head")
    v = lax.axis_index("vocab")
    n_1 = n_v // 4
    core = lax.rem(v, 2)
    p0 = lax.rem(v // 2, 2)
    p1 = v // 4

    def rel(a, b, e):
        return (lax.rem(p1 + a, n_1) * 2 + lax.rem(p0 + b, 2)) * 2 + lax.rem(core + e, 2)

    sib = rel(0, 0, 1)
    x_nb = rel(0, 1, 0)
    queries = q_ref.shape[0]
    keys = k_ref.shape[0]
    context = keys * n_v
    kv_local = k_ref.shape[1] // HD
    heads = kv_local * GROUP
    rows, width = blocks.shape[2], blocks.shape[3]
    half_rows = rows // 2
    voc = u_buf.shape[1]

    w_copy = pltpu.make_async_copy(w_hbm, w_buf, w_sem)
    w_copy.start()
    u_copy = pltpu.make_async_copy(u_hbm, u_buf, u_sem)
    u_copy.start()

    barrier = pltpu.get_barrier_semaphore()
    for j in range(1, n_v):
        pl.semaphore_signal(barrier, inc=1, device_id=(z, lax.rem(v + j, n_v)), device_id_type=MESH)
    for j in range(1, n_h):
        pl.semaphore_signal(barrier, inc=1, device_id=(lax.rem(z + j, n_h), v), device_id_type=MESH)
    pl.semaphore_wait(barrier, n_v - 1 + n_h - 1)

    def kv_copies(j):
        peer = lax.rem(v + j, n_v)
        return [
            pltpu.make_async_remote_copy(
                src_ref=ref, dst_ref=buf.at[v], send_sem=kv_send.at[i, j],
                recv_sem=kv_recv.at[i, v], device_id=(z, peer), device_id_type=MESH,
            )
            for i, (ref, buf) in enumerate(((k_ref, kbuf), (v_ref, vbuf)))
        ]

    def kv_arrived(j):
        peer = lax.rem(v + j, n_v)
        for i, (ref, buf) in enumerate(((k_ref, kbuf), (v_ref, vbuf))):
            pltpu.make_async_remote_copy(
                src_ref=ref, dst_ref=buf.at[peer], send_sem=kv_send.at[i, j],
                recv_sem=kv_recv.at[i, peer], device_id=(z, peer), device_id_type=MESH,
            ).wait_recv()

    for j in range(1, n_v):
        for copy in kv_copies(j):
            copy.start()
    kbuf[v] = k_ref[...]
    vbuf[v] = v_ref[...]

    def block_copy(zp, vp, half, sem, device):
        part = blocks.at[zp, vp, pl.ds(half * half_rows, half_rows)]
        return pltpu.make_async_remote_copy(
            src_ref=part, dst_ref=part, send_sem=sem, recv_sem=recv.at[zp, vp, half],
            device_id=device, device_id_type=MESH,
        )

    def arrived(zp, vp, half):
        block_copy(zp, vp, half, sib_send.at[0, 0, half], (z, sib)).wait_recv()

    def sib_copy(zp, a, b, half):
        return block_copy(zp, rel(a, b, 0), half, sib_send.at[zp, a * 2 + b, half], (z, sib))

    def plane_copies(zp, half):
        return [block_copy(zp, v, half, x_send.at[zp, half], (z, x_nb))] + [
            block_copy(zp, v, half, y_send.at[zp, a, half], (z, rel(a, 0, 0)))
            for a in range(1, n_1)
        ]

    def x_forwards(zp):
        return [
            block_copy(zp, rel(a, 0, 0), 1, x_fwd.at[zp, a], (z, x_nb)) for a in range(1, n_1)
        ]

    def y_forwards(zp):
        return [
            block_copy(zp, x_nb, 0, y_fwd.at[zp, a], (z, rel(a, 0, 0))) for a in range(1, n_1)
        ]

    def along_head(zp, half, act):
        @pl.when((zp <= z) & (z < n_h - 1))
        def _():
            act(block_copy(zp, v, half, z_send.at[zp, 0, half], (z + 1, v)))

        @pl.when((zp >= z) & (z > 0))
        def _():
            act(block_copy(zp, v, half, z_send.at[zp, 1, half], (z - 1, v)))

    def start(copy):
        copy.start()

    def wait_send(copy):
        copy.wait_send()

    def spread(zp, half):
        along_head(zp, half, start)
        for copy in plane_copies(zp, half):
            copy.start()
        sib_copy(zp, 0, 0, half).start()

    query_row = lax.broadcasted_iota(jnp.int32, (queries, context), 0)
    key_pos = lax.broadcasted_iota(jnp.int32, (queries, context), 1)
    row_one = lax.broadcasted_iota(jnp.int32, (queries, 1), 0)
    seen = jnp.zeros((queries, context), jnp.int32)
    scale = jnp.zeros((queries, 1), F32)
    for s in range(queries):
        seen = jnp.where(query_row == s, vis_ref[s], seen)
        scale = jnp.where(row_one == s, fs_ref[s], scale)
    query_pos = context - queries + query_row
    visible_one = ((key_pos <= query_pos) & (key_pos > query_pos - seen)).astype(jnp.int32)
    visible = jnp.concatenate([visible_one] * GROUP, axis=0) > 0

    for j in range(1, n_v):
        kv_arrived(j)
    gap = jnp.zeros((queries, HD), BF16)
    for n in range(kv_local):
        q = jnp.concatenate(
            [q_ref[:, (n * GROUP + g) * HD:(n * GROUP + g + 1) * HD] for g in range(GROUP)], axis=0
        )
        k = kbuf[:, :, n * HD:(n + 1) * HD].reshape(context, HD)
        val = vbuf[:, :, n * HD:(n + 1) * HD].reshape(context, HD)
        scores = lax.dot_general(
            q, k, (((1,), (1,)), ((), ())), preferred_element_type=F32
        ) * HD ** (-0.5)
        masked = jnp.where(visible, scores, NEG_FILL)
        peak = jnp.max(masked, axis=-1, keepdims=True)
        weights = jnp.where(visible, jnp.exp(masked - peak), 0.0)
        total = jnp.sum(weights, axis=-1, keepdims=True)
        high = weights.astype(BF16)
        rest = weights - high.astype(F32)
        mid = rest.astype(BF16)
        low = (rest - mid.astype(F32)).astype(BF16)
        summed = (
            jnp.dot(low, val, preferred_element_type=F32)
            + jnp.dot(mid, val, preferred_element_type=F32)
            + jnp.dot(high, val, preferred_element_type=F32)
        )
        mixed = (summed / total).astype(BF16)
        if n == 0:
            w_copy.wait()
        for g in range(0, GROUP, 2):
            first = mixed[g * queries:(g + 1) * queries]
            second = mixed[(g + 1) * queries:(g + 2) * queries]
            pair = jnp.concatenate(
                [
                    jnp.concatenate([first, gap], axis=1),
                    jnp.concatenate([gap, second], axis=1),
                ],
                axis=0,
            )
            head = n * GROUP + g
            contrib = jnp.dot(
                pair, w_buf[head * HD:(head + 2) * HD], preferred_element_type=F32
            )
            scaled = contrib * jnp.concatenate([scale, scale], axis=0)
            blocks[z, v, pl.ds(head * queries, 2 * queries)] = scaled.astype(BF16)
            if head + 2 == heads // 2:
                spread(z, 0)
            if head + 2 == heads:
                spread(z, 1)

    first_col = (z * n_v + v) * voc
    col = lax.broadcasted_iota(jnp.int32, (queries, voc), 1) + first_col
    voc_row = lax.broadcasted_iota(jnp.int32, (queries, voc), 0)
    wanted = jnp.full((queries, voc), -1, jnp.int32)
    for s in range(queries):
        wanted = jnp.where(voc_row == s, tgt_ref[s], wanted)
    hits = jnp.where(wanted == col, 1.0, 0.0).astype(F32)

    def source(k):
        below, above = z, n_h - 1 - z
        both = jnp.minimum(below, above)
        paired = k <= 2 * both
        distance = jnp.where(paired, (k + 1) // 2, k - both)
        upward = jnp.where(paired, lax.rem(k, 2) == 1, above > below)
        return z + jnp.where(upward, distance, -distance)

    def multiply(zp, vp, fresh=False):
        depth = pl.ds(pl.multiple_of(vp * width, width), width)
        for at, size in column_tiles(voc):
            part = jnp.dot(
                blocks[zp, vp], u_buf[depth, at:at + size], preferred_element_type=F32
            )
            if fresh:
                acc[zp, :, at:at + size] = part
            else:
                acc[zp, :, at:at + size] += part

    def st_copies(zp):
        return [
            pltpu.make_async_remote_copy(
                src_ref=st_all.at[v, zp], dst_ref=st_all.at[v, zp], send_sem=st_send.at[j, zp],
                recv_sem=st_recv.at[v, zp], device_id=(z, lax.rem(v + j, n_v)), device_id_type=MESH,
            )
            for j in range(1, n_v)
        ]

    def finish(zp):
        for a in range(1, n_1):
            for half in range(2):
                arrived(zp, rel(a, 1, 0), half)
                sib_copy(zp, a, 1, half).start()
        for a in range(1, n_1):
            multiply(zp, rel(a, 1, 0))
        for a in range(1, n_1):
            for half in range(2):
                arrived(zp, rel(a, 1, 1), half)
            multiply(zp, rel(a, 1, 1))
        lane = lax.broadcasted_iota(jnp.int32, (2 * queries, HD), 1)
        for at in range(0, rows, 2 * queries):
            logits = acc[zp, at:at + 2 * queries]
            peak = jnp.max(logits, axis=-1, keepdims=True)
            total = jnp.sum(jnp.exp(logits - peak), axis=-1, keepdims=True)
            picked = jnp.sum(
                logits * jnp.concatenate([hits, hits], axis=0), axis=-1, keepdims=True
            )
            cols[at:at + 2 * queries] = jnp.where(
                lane == 0, peak, jnp.where(lane == 1, total, picked)
            )
        st_all[v, zp] = cols[...].T[:8]
        for copy in st_copies(zp):
            copy.start()

    u_copy.wait()

    def step(k, carry):
        zk = source(k)
        after = source(k + 1)
        for half in range(2):
            @pl.when(k + 1 < n_h)
            def _():
                arrived(after, v, half)
                spread(after, half)

            if half == 0:
                multiply(zk, v, fresh=True)
            arrived(zk, x_nb, half)
            if half == 0:
                for copy in y_forwards(zk):
                    copy.start()
            sib_copy(zk, 0, 1, half).start()
            for a in range(1, n_1):
                arrived(zk, rel(a, 0, 0), half)
            if half == 1:
                for copy in x_forwards(zk):
                    copy.start()
            for a in range(1, n_1):
                sib_copy(zk, a, 0, half).start()

        multiply(zk, x_nb)
        for a in range(1, n_1):
            multiply(zk, rel(a, 0, 0))
        for a, b in [(0, 0), (0, 1)] + [(a, 0) for a in range(1, n_1)]:
            for half in range(2):
                arrived(zk, rel(a, b, 1), half)
            multiply(zk, rel(a, b, 1))

        @pl.when(k > 0)
        def _():
            finish(source(k - 1))

        return carry

    lax.fori_loop(0, n_h, step, 0)
    finish(source(n_h - 1))

    def st_wait(j, zp):
        peer = lax.rem(v + j, n_v)
        pltpu.make_async_remote_copy(
            src_ref=st_all.at[peer, zp], dst_ref=st_all.at[peer, zp], send_sem=st_send.at[j, zp],
            recv_sem=st_recv.at[peer, zp], device_id=(z, peer), device_id_type=MESH,
        ).wait_recv()

    for j in range(1, n_v):
        for zp in range(n_h):
            st_wait(j, zp)

    def merged(parts):
        peak = functools.reduce(jnp.maximum, [part[:, 0:1] for part in parts])
        total = sum(part[:, 1:2] * jnp.exp(part[:, 0:1] - peak) for part in parts)
        picked = sum(part[:, 2:3] for part in parts)
        return peak, total, picked

    peak, total, picked = merged([st_all[i] for i in range(n_v)])
    st_z[z] = jnp.concatenate([peak, total, picked, jnp.zeros((n_h, 5, rows), F32)], axis=1)

    def sz_copy(j, slot):
        peer = lax.rem(z + j, n_h)
        return pltpu.make_async_remote_copy(
            src_ref=st_z.at[slot], dst_ref=st_z.at[slot], send_sem=sz_send.at[j],
            recv_sem=sz_recv.at[slot], device_id=(peer, v), device_id_type=MESH,
        )

    for j in range(1, n_h):
        sz_copy(j, z).start()
    for j in range(1, n_h):
        sz_copy(j, lax.rem(z + j, n_h)).wait_recv()
    peak, total, picked = merged([st_z[i] for i in range(n_h)])
    tl_ref[...] = picked
    ln_ref[...] = peak + jnp.log(total)

    for j in range(1, n_h):
        sz_copy(j, z).wait_send()
    for j in range(1, n_v):
        for copy in kv_copies(j):
            copy.wait_send()

    def drain(zp, carry):
        for half in range(2):
            along_head(zp, half, wait_send)
            for copy in plane_copies(zp, half):
                copy.wait_send()
            for a in range(n_1):
                for b in range(2):
                    sib_copy(zp, a, b, half).wait_send()
        for copy in x_forwards(zp) + y_forwards(zp) + st_copies(zp):
            copy.wait_send()
        return carry

    lax.fori_loop(0, n_h, drain, 0)


def solution(mesh):
    n_h, n_v = mesh.shape["head"], mesh.shape["vocab"]

    def body(queries, key_cache, value_cache, visible_len, targets, final_scale, w_out, unembed):
        count = queries.shape[0]
        rows = w_out.shape[0] // HD * count
        width = w_out.shape[1]
        voc = unembed.shape[1]
        n_1 = n_v // 4
        smem = pl.BlockSpec(memory_space=pltpu.SMEM)
        vmem = pl.BlockSpec(memory_space=pltpu.VMEM)
        hbm = pl.BlockSpec(memory_space=pl.ANY)
        dma = pltpu.SemaphoreType.DMA
        target_logit, log_norm = pl.pallas_call(
            functools.partial(kernel, n_h, n_v),
            out_shape=[jax.ShapeDtypeStruct((n_h, 1, rows), F32)] * 2,
            in_specs=[smem, smem, smem, vmem, vmem, vmem, hbm, hbm],
            out_specs=[vmem, vmem],
            scratch_shapes=[
                pltpu.VMEM(w_out.shape, BF16),
                pltpu.VMEM(unembed.shape, BF16),
                pltpu.VMEM((n_h, n_v, rows, width), BF16),
                pltpu.VMEM((n_h, rows, voc), F32),
                pltpu.VMEM((n_v,) + key_cache.shape, BF16),
                pltpu.VMEM((n_v,) + value_cache.shape, BF16),
                pltpu.VMEM((rows, HD), F32),
                pltpu.VMEM((n_v, n_h, 8, rows), F32),
                pltpu.VMEM((n_h, n_h, 8, rows), F32),
                dma,
                dma,
                dma((2, n_v)),
                dma((2, n_v)),
                dma((n_h, n_v, 2)),
                dma((n_h, 2, 2)),
                dma((n_h, 2)),
                dma((n_h, n_1, 2)),
                dma((n_h, n_1)),
                dma((n_h, n_1)),
                dma((n_h, n_v // 2, 2)),
                dma((n_v, n_h)),
                dma((n_v, n_h)),
                dma((n_h,)),
                dma((n_h,)),
            ],
            compiler_params=pltpu.CompilerParams(
                collective_id=0, has_side_effects=True, vmem_limit_bytes=58 * 2 ** 20
            ),
        )(visible_len, targets, final_scale, queries, key_cache, value_cache, w_out, unembed)
        return target_logit.reshape(H, count), log_norm.reshape(H, count)

    return jax.shard_map(
        body,
        mesh=mesh,
        in_specs=(
            P(None, "head"),
            P("vocab", "head"),
            P("vocab", "head"),
            P(),
            P(),
            P(),
            P("head", "vocab"),
            P(None, ("head", "vocab")),
        ),
        out_specs=(P(), P()),
        check_vma=False,
    )
```

```python
import functools

import jax
import jax.numpy as jnp
from jax import lax
from jax.experimental import pallas as pl
from jax.experimental.pallas import tpu as pltpu
from jax.sharding import PartitionSpec as P

H = 64
KVH = 8
HD = 128
GROUP = H // KVH
NEG_FILL = -1e30
MESH = pl.DeviceIdType.MESH
F32 = jnp.float32
BF16 = jnp.bfloat16


def column_tiles(width, tile=256):
    return [(at, min(tile, width - at)) for at in range(0, width, tile)]


def kernel(
    n_h, n_v,
    vis_ref, tgt_ref, fs_ref, q_ref, k_ref, v_ref, w_hbm, u_hbm,
    tl_ref, ln_ref,
    w_buf, u_buf, blocks, acc, kbuf, vbuf, cols, st_all, st_z,
    w_sem, u_sem, kv_send, kv_recv, recv, z_send, x_send, y_send, x_fwd, y_fwd, sib_send, diag_send,
    st_send, st_recv, sz_send, sz_recv,
):
    z = lax.axis_index("head")
    v = lax.axis_index("vocab")
    n_1 = n_v // 4
    core = lax.rem(v, 2)
    p0 = lax.rem(v // 2, 2)
    p1 = v // 4

    def rel(a, b, e):
        return (lax.rem(p1 + a, n_1) * 2 + lax.rem(p0 + b, 2)) * 2 + lax.rem(core + e, 2)

    sib = rel(0, 0, 1)
    x_nb = rel(0, 1, 0)
    queries = q_ref.shape[0]
    keys = k_ref.shape[0]
    context = keys * n_v
    kv_local = k_ref.shape[1] // HD
    heads = kv_local * GROUP
    rows, width = blocks.shape[2], blocks.shape[3]
    half_rows = rows // 2
    voc = u_buf.shape[1]

    w_copy = pltpu.make_async_copy(w_hbm, w_buf, w_sem)
    w_copy.start()
    u_copy = pltpu.make_async_copy(u_hbm, u_buf, u_sem)
    u_copy.start()

    barrier = pltpu.get_barrier_semaphore()
    for j in range(1, n_v):
        pl.semaphore_signal(barrier, inc=1, device_id=(z, lax.rem(v + j, n_v)), device_id_type=MESH)
    for j in range(1, n_h):
        pl.semaphore_signal(barrier, inc=1, device_id=(lax.rem(z + j, n_h), v), device_id_type=MESH)
    pl.semaphore_wait(barrier, n_v - 1 + n_h - 1)

    def kv_copies(j):
        peer = lax.rem(v + j, n_v)
        return [
            pltpu.make_async_remote_copy(
                src_ref=ref, dst_ref=buf.at[v], send_sem=kv_send.at[i, j],
                recv_sem=kv_recv.at[i, v], device_id=(z, peer), device_id_type=MESH,
            )
            for i, (ref, buf) in enumerate(((k_ref, kbuf), (v_ref, vbuf)))
        ]

    def kv_arrived(j):
        peer = lax.rem(v + j, n_v)
        for i, (ref, buf) in enumerate(((k_ref, kbuf), (v_ref, vbuf))):
            pltpu.make_async_remote_copy(
                src_ref=ref, dst_ref=buf.at[peer], send_sem=kv_send.at[i, j],
                recv_sem=kv_recv.at[i, peer], device_id=(z, peer), device_id_type=MESH,
            ).wait_recv()

    for j in range(1, n_v):
        for copy in kv_copies(j):
            copy.start()
    kbuf[v] = k_ref[...]
    vbuf[v] = v_ref[...]

    def block_copy(zp, vp, half, sem, device):
        part = blocks.at[zp, vp, pl.ds(half * half_rows, half_rows)]
        return pltpu.make_async_remote_copy(
            src_ref=part, dst_ref=part, send_sem=sem, recv_sem=recv.at[zp, vp, half],
            device_id=device, device_id_type=MESH,
        )

    def arrived(zp, vp, half):
        block_copy(zp, vp, half, sib_send.at[0, 0, half], (z, sib)).wait_recv()

    def sib_copy(zp, a, b, half):
        return block_copy(zp, rel(a, b, 0), half, sib_send.at[zp, a * 2 + b, half], (z, sib))

    def plane_copies(zp, half):
        return [block_copy(zp, v, half, x_send.at[zp, half], (z, x_nb))] + [
            block_copy(zp, v, half, y_send.at[zp, a, half], (z, rel(a, 0, 0)))
            for a in range(1, n_1)
        ]

    def x_forwards(zp):
        return [
            block_copy(zp, rel(a, 0, 0), 1, x_fwd.at[zp, a], (z, x_nb)) for a in range(1, n_1)
        ]

    def y_forwards(zp):
        return [
            block_copy(zp, x_nb, 0, y_fwd.at[zp, a], (z, rel(a, 0, 0))) for a in range(1, n_1)
        ]

    def along_head(zp, half, act):
        @pl.when((zp <= z) & (z < n_h - 1))
        def _():
            act(block_copy(zp, v, half, z_send.at[zp, 0, half], (z + 1, v)))

        @pl.when((zp >= z) & (z > 0))
        def _():
            act(block_copy(zp, v, half, z_send.at[zp, 1, half], (z - 1, v)))

    def apart(zp):
        return jnp.where(zp > z, zp - z, z - zp)

    def over_plane(zp):
        return (apart(zp) == 0) | (apart(zp) > 2)

    def diagonal_along_head(zp, a, half, act):
        vp = rel(a, 1, 0)

        @pl.when((zp <= z) & (z < n_h - 1) & (apart(zp) < 2))
        def _():
            act(block_copy(zp, vp, half, diag_send.at[zp, a, half], (z + 1, v)))

        @pl.when((zp >= z) & (z > 0) & (apart(zp) < 2))
        def _():
            act(block_copy(zp, vp, half, diag_send.at[zp, n_1 + a, half], (z - 1, v)))

    def start(copy):
        copy.start()

    def wait_send(copy):
        copy.wait_send()

    def spread(zp, half):
        along_head(zp, half, start)
        for copy in plane_copies(zp, half):
            copy.start()
        sib_copy(zp, 0, 0, half).start()

    query_row = lax.broadcasted_iota(jnp.int32, (queries, context), 0)
    key_pos = lax.broadcasted_iota(jnp.int32, (queries, context), 1)
    row_one = lax.broadcasted_iota(jnp.int32, (queries, 1), 0)
    seen = jnp.zeros((queries, context), jnp.int32)
    scale = jnp.zeros((queries, 1), F32)
    for s in range(queries):
        seen = jnp.where(query_row == s, vis_ref[s], seen)
        scale = jnp.where(row_one == s, fs_ref[s], scale)
    query_pos = context - queries + query_row
    visible_one = ((key_pos <= query_pos) & (key_pos > query_pos - seen)).astype(jnp.int32)
    visible = jnp.concatenate([visible_one] * GROUP, axis=0) > 0

    for j in range(1, n_v):
        kv_arrived(j)
    gap = jnp.zeros((queries, HD), BF16)
    for n in range(kv_local):
        q = jnp.concatenate(
            [q_ref[:, (n * GROUP + g) * HD:(n * GROUP + g + 1) * HD] for g in range(GROUP)], axis=0
        )
        k = kbuf[:, :, n * HD:(n + 1) * HD].reshape(context, HD)
        val = vbuf[:, :, n * HD:(n + 1) * HD].reshape(context, HD)
        scores = lax.dot_general(
            q, k, (((1,), (1,)), ((), ())), preferred_element_type=F32
        ) * HD ** (-0.5)
        masked = jnp.where(visible, scores, NEG_FILL)
        peak = jnp.max(masked, axis=-1, keepdims=True)
        weights = jnp.where(visible, jnp.exp(masked - peak), 0.0)
        total = jnp.sum(weights, axis=-1, keepdims=True)
        high = weights.astype(BF16)
        rest = weights - high.astype(F32)
        mid = rest.astype(BF16)
        low = (rest - mid.astype(F32)).astype(BF16)
        summed = (
            jnp.dot(low, val, preferred_element_type=F32)
            + jnp.dot(mid, val, preferred_element_type=F32)
            + jnp.dot(high, val, preferred_element_type=F32)
        )
        mixed = (summed / total).astype(BF16)
        if n == 0:
            w_copy.wait()
        for g in range(0, GROUP, 2):
            first = mixed[g * queries:(g + 1) * queries]
            second = mixed[(g + 1) * queries:(g + 2) * queries]
            pair = jnp.concatenate(
                [
                    jnp.concatenate([first, gap], axis=1),
                    jnp.concatenate([gap, second], axis=1),
                ],
                axis=0,
            )
            head = n * GROUP + g
            contrib = jnp.dot(
                pair, w_buf[head * HD:(head + 2) * HD], preferred_element_type=F32
            )
            scaled = contrib * jnp.concatenate([scale, scale], axis=0)
            blocks[z, v, pl.ds(head * queries, 2 * queries)] = scaled.astype(BF16)
            if head + 2 == heads // 2:
                spread(z, 0)
            if head + 2 == heads:
                spread(z, 1)

    first_col = (z * n_v + v) * voc
    col = lax.broadcasted_iota(jnp.int32, (queries, voc), 1) + first_col
    voc_row = lax.broadcasted_iota(jnp.int32, (queries, voc), 0)
    wanted = jnp.full((queries, voc), -1, jnp.int32)
    for s in range(queries):
        wanted = jnp.where(voc_row == s, tgt_ref[s], wanted)
    hits = jnp.where(wanted == col, 1.0, 0.0).astype(F32)

    def source(k):
        below, above = z, n_h - 1 - z
        both = jnp.minimum(below, above)
        paired = k <= 2 * both
        distance = jnp.where(paired, (k + 1) // 2, k - both)
        upward = jnp.where(paired, lax.rem(k, 2) == 1, above > below)
        return z + jnp.where(upward, distance, -distance)

    def multiply(zp, vp, fresh=False):
        depth = pl.ds(pl.multiple_of(vp * width, width), width)
        for at, size in column_tiles(voc):
            part = jnp.dot(
                blocks[zp, vp], u_buf[depth, at:at + size], preferred_element_type=F32
            )
            if fresh:
                acc[zp, :, at:at + size] = part
            else:
                acc[zp, :, at:at + size] += part

    def st_copies(zp):
        return [
            pltpu.make_async_remote_copy(
                src_ref=st_all.at[v, zp], dst_ref=st_all.at[v, zp], send_sem=st_send.at[j, zp],
                recv_sem=st_recv.at[v, zp], device_id=(z, lax.rem(v + j, n_v)), device_id_type=MESH,
            )
            for j in range(1, n_v)
        ]

    def finish(zp):
        for a in range(1, n_1):
            for half in range(2):
                arrived(zp, rel(a, 1, 0), half)
                diagonal_along_head(zp, a, half, start)
                sib_copy(zp, a, 1, half).start()
        for a in range(1, n_1):
            multiply(zp, rel(a, 1, 0))
        for a in range(1, n_1):
            for half in range(2):
                arrived(zp, rel(a, 1, 1), half)
            multiply(zp, rel(a, 1, 1))
        lane = lax.broadcasted_iota(jnp.int32, (2 * queries, HD), 1)
        for at in range(0, rows, 2 * queries):
            logits = acc[zp, at:at + 2 * queries]
            peak = jnp.max(logits, axis=-1, keepdims=True)
            total = jnp.sum(jnp.exp(logits - peak), axis=-1, keepdims=True)
            picked = jnp.sum(
                logits * jnp.concatenate([hits, hits], axis=0), axis=-1, keepdims=True
            )
            cols[at:at + 2 * queries] = jnp.where(
                lane == 0, peak, jnp.where(lane == 1, total, picked)
            )
        st_all[v, zp] = cols[...].T[:8]
        for copy in st_copies(zp):
            copy.start()

    u_copy.wait()

    def step(k, carry):
        zk = source(k)
        after = source(k + 1)
        for half in range(2):
            @pl.when(k + 1 < n_h)
            def _():
                arrived(after, v, half)
                spread(after, half)

            if half == 0:
                multiply(zk, v, fresh=True)
            arrived(zk, x_nb, half)
            if half == 0:
                @pl.when(over_plane(zk))
                def _():
                    for copy in y_forwards(zk):
                        copy.start()

            sib_copy(zk, 0, 1, half).start()
            for a in range(1, n_1):
                arrived(zk, rel(a, 0, 0), half)
            if half == 1:
                @pl.when(over_plane(zk))
                def _():
                    for copy in x_forwards(zk):
                        copy.start()

            for a in range(1, n_1):
                sib_copy(zk, a, 0, half).start()

        multiply(zk, x_nb)
        for a in range(1, n_1):
            multiply(zk, rel(a, 0, 0))
        for a, b in [(0, 0), (0, 1)] + [(a, 0) for a in range(1, n_1)]:
            for half in range(2):
                arrived(zk, rel(a, b, 1), half)
            multiply(zk, rel(a, b, 1))

        @pl.when(k > 0)
        def _():
            finish(source(k - 1))

        return carry

    lax.fori_loop(0, n_h, step, 0)
    finish(source(n_h - 1))

    def st_wait(j, zp):
        peer = lax.rem(v + j, n_v)
        pltpu.make_async_remote_copy(
            src_ref=st_all.at[peer, zp], dst_ref=st_all.at[peer, zp], send_sem=st_send.at[j, zp],
            recv_sem=st_recv.at[peer, zp], device_id=(z, peer), device_id_type=MESH,
        ).wait_recv()

    for j in range(1, n_v):
        for zp in range(n_h):
            st_wait(j, zp)

    def merged(parts):
        peak = functools.reduce(jnp.maximum, [part[:, 0:1] for part in parts])
        total = sum(part[:, 1:2] * jnp.exp(part[:, 0:1] - peak) for part in parts)
        picked = sum(part[:, 2:3] for part in parts)
        return peak, total, picked

    peak, total, picked = merged([st_all[i] for i in range(n_v)])
    st_z[z] = jnp.concatenate([peak, total, picked, jnp.zeros((n_h, 5, rows), F32)], axis=1)

    def sz_copy(j, slot):
        peer = lax.rem(z + j, n_h)
        return pltpu.make_async_remote_copy(
            src_ref=st_z.at[slot], dst_ref=st_z.at[slot], send_sem=sz_send.at[j],
            recv_sem=sz_recv.at[slot], device_id=(peer, v), device_id_type=MESH,
        )

    for j in range(1, n_h):
        sz_copy(j, z).start()
    for j in range(1, n_h):
        sz_copy(j, lax.rem(z + j, n_h)).wait_recv()
    peak, total, picked = merged([st_z[i] for i in range(n_h)])
    norm = peak + jnp.log(total)
    for i in range(n_h):
        tl_ref[i:i + 1] = picked[i]
        ln_ref[i:i + 1] = norm[i]

    for j in range(1, n_h):
        sz_copy(j, z).wait_send()
    for j in range(1, n_v):
        for copy in kv_copies(j):
            copy.wait_send()

    def drain(zp, carry):
        for half in range(2):
            along_head(zp, half, wait_send)
            for copy in plane_copies(zp, half):
                copy.wait_send()
            for a in range(n_1):
                for b in range(2):
                    sib_copy(zp, a, b, half).wait_send()
            for a in range(1, n_1):
                diagonal_along_head(zp, a, half, wait_send)

        @pl.when(over_plane(zp))
        def _():
            for copy in x_forwards(zp) + y_forwards(zp):
                copy.wait_send()

        for copy in st_copies(zp):
            copy.wait_send()
        return carry

    lax.fori_loop(0, n_h, drain, 0)


def solution(mesh):
    n_h, n_v = mesh.shape["head"], mesh.shape["vocab"]

    def body(queries, key_cache, value_cache, visible_len, targets, final_scale, w_out, unembed):
        count = queries.shape[0]
        rows = w_out.shape[0] // HD * count
        width = w_out.shape[1]
        voc = unembed.shape[1]
        n_1 = n_v // 4
        smem = pl.BlockSpec(memory_space=pltpu.SMEM)
        vmem = pl.BlockSpec(memory_space=pltpu.VMEM)
        hbm = pl.BlockSpec(memory_space=pl.ANY)
        dma = pltpu.SemaphoreType.DMA
        target_logit, log_norm = pl.pallas_call(
            functools.partial(kernel, n_h, n_v),
            out_shape=[jax.ShapeDtypeStruct((n_h, rows), F32)] * 2,
            in_specs=[smem, smem, smem, vmem, vmem, vmem, hbm, hbm],
            out_specs=[vmem, vmem],
            scratch_shapes=[
                pltpu.VMEM(w_out.shape, BF16),
                pltpu.VMEM(unembed.shape, BF16),
                pltpu.VMEM((n_h, n_v, rows, width), BF16),
                pltpu.VMEM((n_h, rows, voc), F32),
                pltpu.VMEM((n_v,) + key_cache.shape, BF16),
                pltpu.VMEM((n_v,) + value_cache.shape, BF16),
                pltpu.VMEM((rows, HD), F32),
                pltpu.VMEM((n_v, n_h, 8, rows), F32),
                pltpu.VMEM((n_h, n_h, 8, rows), F32),
                dma,
                dma,
                dma((2, n_v)),
                dma((2, n_v)),
                dma((n_h, n_v, 2)),
                dma((n_h, 2, 2)),
                dma((n_h, 2)),
                dma((n_h, n_1, 2)),
                dma((n_h, n_1)),
                dma((n_h, n_1)),
                dma((n_h, n_v // 2, 2)),
                dma((n_h, 2 * n_1, 2)),
                dma((n_v, n_h)),
                dma((n_v, n_h)),
                dma((n_h,)),
                dma((n_h,)),
            ],
            compiler_params=pltpu.CompilerParams(
                collective_id=0, has_side_effects=True, vmem_limit_bytes=58 * 2 ** 20
            ),
        )(visible_len, targets, final_scale, queries, key_cache, value_cache, w_out, unembed)
        return target_logit.reshape(H, count), log_norm.reshape(H, count)

    return jax.shard_map(
        body,
        mesh=mesh,
        in_specs=(
            P(None, "head"),
            P("vocab", "head"),
            P("vocab", "head"),
            P(),
            P(),
            P(),
            P("head", "vocab"),
            P(None, ("head", "vocab")),
        ),
        out_specs=(P(), P()),
        check_vma=False,
    )
```
